32 devices in a mesh: groups: 2 (over x), dp: 4 (over z), tensor: 4 (over y, core).
Axes of the slice: x: 2, y: 2, z: 4, core: 2. Of those that a mesh axis runs over, the one named last changes fastest.
Arguments:
- hidden_input: bfloat16 [4096, 5120], P(('groups', 'dp', 'tensor')), parts along dimension 0, may hold values from -0.119628906 to 0.119628906
- query_gradient: bfloat16 [4096, 8192], P(('groups', 'dp'), 'tensor'), parts along dimension 0, may hold values from -6 to 6
- weight: bfloat16 [5120, 8192], P(None, 'tensor'), may hold values from -0.078125 to 0.078125
- adapter_down: bfloat16 [8, 5120, 64], P(None, 'tensor'), may hold values from -0.078125 to 0.078125
- adapter_up: bfloat16 [8, 64, 8192], P(None, None, 'tensor'), may hold values from -0.0625 to 0.0625
- live_per_block: int32 [32], P(('groups', 'dp')), parts along dimension 0, may hold values from 1 to 128, 1536 in all
- adapter_per_block: int32 [32, 1], P(('groups', 'dp')), parts along dimension 0, may hold values from 0 to 7
Outputs:
- hidden_gradient: bfloat16 [4096, 5120], P(('groups', 'dp', 'tensor')), parts along dimension 0
- grad_down: float32 [16, 5120, 64], P(('groups', 'dp'), 'tensor'), parts along dimension 0
- grad_up: float32 [16, 64, 8192], P(('groups', 'dp'), None, 'tensor'), parts along dimension 0
The draws below stay inside these ranges and needn't reach their ends.
There are 2 independent parts, one for each index of `groups`. The reference program is written for one: setup_inputs(seed, part) draws one part's arguments, and reference() takes and returns one part's arrays. A program takes and returns all parts, laid end to end along the dimension named above; an argument that names none is the same for every part. Nothing has to cross between parts.
Inputs may be any that keep to these rules, and one draw needn't show every extreme that they name: live_per_block gives how many rows at the head of a block of 128 rows are live; some block is full. `adapter_per_block`: every adapter owns some block.
All inputs are finite; a program needn't handle non-finite values.
Results may differ from the reference program's by a relative error of at most 0.015.
Values may be sent and summed in bfloat16 or wider, within the bound.
A program may use at most 128 MiB of HBM per device.

```python
import math
import jax
import jax.numpy as jnp
import numpy as np
from jax import lax

MODEL_WIDTH = 5120
QUERY_WIDTH = 8192
ADAPTER_RANK = 64
BLOCK = 128
ADAPTER_COUNT = 8
TOKEN_ROWS = 2048
NBLK = 16
N_TENSOR = 4


def levels(stream_key, dims, pieces, smallest, top_value):
    loudness = 1.0
    for dim, blocks in pieces:
        steps = jax.random.uniform(jax.random.fold_in(jax.random.fold_in(stream_key, 6), dim), (blocks,), jnp.float32, smallest / len(pieces), top_value / len(pieces))
        loudness = loudness * jnp.repeat(jnp.exp(steps), dims[dim] // blocks).reshape((-1,) + (1,) * (len(dims) - 1 - dim))
    return loudness


def different_ones(stream_key, rows, number_of, top, lift):
    order = jax.random.permutation(jax.random.fold_in(stream_key, 1), number_of)
    favour = order
    for power in range(3):
        favour = favour * favour // number_of
    favour = favour * lift // number_of
    lots = jax.random.randint(jax.random.fold_in(stream_key, 2), (rows, number_of), 0, 4096) + favour
    sure = jax.random.permutation(jax.random.fold_in(stream_key, 3), rows)[jnp.arange(number_of) % rows]
    lots = jnp.where(jnp.arange(rows)[:, None] == sure[None, :], 1 << 14, lots)
    score = lots * number_of + jnp.arange(number_of)
    return lax.top_k(score.astype(jnp.int32), top)[1].astype(jnp.int32)


def profile(count, total, bound, skew):
    weights = [(1 << 20) // math.isqrt(grade ** skew) + 1 for grade in range(2, count + 1)]
    rest, given = total - bound - (count - 1), [1] * (count - 1)
    while rest > 0:
        movable = [i for i in range(count - 1) if given[i] < bound]
        pool, left = sum([weights[i] for i in movable]), rest
        for i in movable:
            more = min(bound - given[i], max(1, left * weights[i] // pool), rest)
            given[i] = given[i] + more
            rest = rest - more
    return np.array([bound] + given)


def ragged(own_key, count, total, bound, slope):
    if count == 2:
        one = jax.random.randint(own_key, (), max(1, total - bound), min(bound, total - 1) + 1)
        return jnp.stack([one, total - one])
    tallies = jnp.asarray(profile(count, total, bound, slope), jnp.int32)
    couples = (count - 1) // 2
    source_of, receiver = tallies[1:1 + 2 * couples:2], tallies[2:2 + 2 * couples:2]
    margin = jnp.minimum(source_of - 1, bound - receiver)
    passed = jax.random.randint(jax.random.fold_in(own_key, 1), (couples,), 0, 1 << 20) % (margin + 1)
    tallies = tallies.at[1:1 + 2 * couples:2].set(source_of - passed).at[2:2 + 2 * couples:2].set(receiver + passed)
    return tallies[jax.random.permutation(jax.random.fold_in(own_key, 2), count)]


def noise(own_key, shape, scale, bound, cuts=(), held_as=jnp.bfloat16):
    result = jax.random.normal(own_key, shape, jnp.float32) * scale
    if len(cuts) > 0:
        result = levels(own_key, shape, cuts, -0.22, 0.18) * result
    return jnp.clip(result, min=-bound, max=bound).astype(held_as)


def setup_inputs(seed: int = 0, part: int = 0) -> dict:
    arg_keys = jax.random.split(jax.random.key(seed), 8)
    own_keys = jax.random.split(jax.random.fold_in(arg_keys[7], part), 8)
    hidden_input = noise(own_keys[0], (TOKEN_ROWS, MODEL_WIDTH), 0.02, 0.119628906, ((0, 16),))
    query_gradient = noise(own_keys[1], (TOKEN_ROWS, QUERY_WIDTH), 1.0, 6.0, ((0, 4), (1, 4)))
    weight = noise(arg_keys[2], (MODEL_WIDTH, QUERY_WIDTH), MODEL_WIDTH ** -0.5, 0.078125, ((1, 4),))
    adapter_down = noise(arg_keys[3], (ADAPTER_COUNT, MODEL_WIDTH, ADAPTER_RANK), MODEL_WIDTH ** -0.5, 0.078125, ((1, 4),))
    adapter_up = noise(arg_keys[4], (ADAPTER_COUNT, ADAPTER_RANK, QUERY_WIDTH), QUERY_WIDTH ** -0.5, 0.0625, ((2, 4),))
    live_per_block = ragged(own_keys[5], NBLK, NBLK * 96, BLOCK, 0).astype(jnp.int32)
    adapter_per_block = different_ones(own_keys[6], NBLK, ADAPTER_COUNT, 1, 2048)
    return dict(hidden_input=hidden_input, query_gradient=query_gradient, weight=weight, adapter_down=adapter_down, adapter_up=adapter_up, live_per_block=live_per_block, adapter_per_block=adapter_per_block)


adapter_scale = 2.0


def reference(hidden_input, query_gradient, weight, adapter_down, adapter_up, live_per_block, adapter_per_block):
    positions = jnp.arange(BLOCK, dtype=jnp.int32)
    live = (positions[None, :] < live_per_block[:, None]).astype(jnp.bfloat16)
    masked_rows = query_gradient.reshape(NBLK, BLOCK, QUERY_WIDTH) * live[:, :, None]
    flat = masked_rows.reshape(TOKEN_ROWS, QUERY_WIDTH)
    width = QUERY_WIDTH // N_TENSOR
    w_parts = weight.reshape(MODEL_WIDTH, N_TENSOR, width).transpose(1, 0, 2)
    g_parts = flat.reshape(TOKEN_ROWS, N_TENSOR, width).transpose(1, 0, 2)

    def add_part(total, pair):
        g_piece, w_piece = pair
        part = lax.dot_general(g_piece, w_piece, (((1,), (1,)), ((), ())), preferred_element_type=jnp.float32)
        return total + part.astype(jnp.bfloat16).astype(jnp.float32), None

    frozen_gradient, _ = lax.scan(add_part, jnp.zeros((TOKEN_ROWS, MODEL_WIDTH), jnp.float32), (g_parts, w_parts))
    adapter_index = adapter_per_block[:, 0].astype(jnp.int32)
    hidden_block_list = hidden_input.reshape(NBLK, BLOCK, MODEL_WIDTH)

    def single_block(carry, item):
        down_running, up_running = carry
        grad_blk, hid_blk, block_index = item
        down_matrix = adapter_down[block_index]
        up_matrix = adapter_up[block_index]
        low_grad = lax.dot_general(grad_blk, up_matrix, (((1,), (1,)), ((), ())), preferred_element_type=jnp.float32)
        low_act = jnp.dot(hid_blk, down_matrix, preferred_element_type=jnp.float32)
        gradient_batch = low_grad.astype(jnp.bfloat16)
        act_b = low_act.astype(jnp.bfloat16)
        adapter_rows = (adapter_scale * lax.dot_general(gradient_batch, down_matrix, (((1,), (1,)), ((), ())), preferred_element_type=jnp.float32)).astype(jnp.bfloat16)
        down_term = lax.dot_general(hid_blk, gradient_batch, (((0,), (0,)), ((), ())), preferred_element_type=jnp.float32)
        up_term = lax.dot_general(act_b, grad_blk, (((0,), (0,)), ((), ())), preferred_element_type=jnp.float32)
        down_running = down_running.at[block_index].add(down_term)
        up_running = up_running.at[block_index].add(up_term)
        return (down_running, up_running), adapter_rows

    start_row = (jnp.zeros((ADAPTER_COUNT, MODEL_WIDTH, ADAPTER_RANK), jnp.float32), jnp.zeros((ADAPTER_COUNT, ADAPTER_RANK, QUERY_WIDTH), jnp.float32))
    (down_running, up_running), adapter_gradient = lax.scan(single_block, start_row, (masked_rows, hidden_block_list, adapter_index))
    hidden_gradient = (frozen_gradient + adapter_gradient.reshape(TOKEN_ROWS, MODEL_WIDTH).astype(jnp.float32)).astype(jnp.bfloat16)
    return hidden_gradient, adapter_scale * down_running, adapter_scale * up_running
```

```python
import jax
import jax.numpy as jnp
from jax import lax
from jax.experimental import pallas as pl
from jax.experimental.pallas import tpu as pltpu
from jax.sharding import PartitionSpec as P

BLOCK = 128
MESH = pl.DeviceIdType.MESH
F32, BF16 = jnp.float32, jnp.bfloat16


adapter_scale = 2.0
UP_CHUNKS, DOWN_CHUNKS, STEP, WBUFS = 4, 2, 256, 3


def dot_nt(a, b):
    return lax.dot_general(a, b, (((1,), (1,)), ((), ())), preferred_element_type=F32)


def dot_nn(a, b):
    return lax.dot_general(a, b, (((1,), (0,)), ((), ())), preferred_element_type=F32)


def dot_tn(a, b):
    return lax.dot_general(a, b, (((0,), (0,)), ((), ())), preferred_element_type=F32)


def kernel(
    live_ref, idx_ref, hid_ref, g_ref, w_ref, down_ref, up_ref,
    hg_ref, gd_ref, gu_ref,
    m_g, w_buf, up_v, down_v, cols, pf, acc, core_s, core_r, y_s, y_r, lora,
    lg_s, lg_r, la_s, la_r, low_g, low_a, lhs, slots_d, slots_u,
    s1d, s1u, td, tu, xd, xu, s2d, s2u, fd, fu, ids_s, ids_r, sel,
    loc_sem, w_sem, hs_sem, hr_sem, lgs_sem, lgr_sem, las_sem, lar_sem,
    cs_sem, cr_sem, ys_sem, yr_sem,
    s1_sem, t_sem, x_sem, s2_sem, f_sem, id_sem,
):
    d = lax.axis_index("dp")
    t = lax.axis_index("tensor")
    y, c = t // 2, t % 2
    core_peer = y * 2 + (1 - c)
    y_peer = (1 - y) * 2 + c
    is_mid = jnp.logical_or(d == 1, d == 2)
    is_end = jnp.logical_not(is_mid)
    low_side = d < 2
    outer = jnp.where(low_side, 0, 3)
    inner = jnp.where(low_side, 1, 2)
    cross = jnp.where(low_side, 2, 1)
    far = 3 - outer
    nb = 4
    own, rank = gd_ref.shape[0] // 64, 64
    width = down_v.shape[2]
    q = m_g.shape[1]
    uw, dw = q // UP_CHUNKS, width // DOWN_CHUNKS

    loads = [
        pltpu.make_async_copy(g_ref, m_g, loc_sem.at[0]),
        pltpu.make_async_copy(up_ref, up_v, loc_sem.at[1]),
        pltpu.make_async_copy(hid_ref.at[:, pl.ds(pl.multiple_of(t * width, 128), width)],
                              cols.at[pl.ds(pl.multiple_of(t * BLOCK, BLOCK), BLOCK), :], loc_sem.at[2]),
        pltpu.make_async_copy(down_ref, down_v, loc_sem.at[3]),
    ]
    for x in loads[:2]:
        x.start()

    def w_load(j):
        return pltpu.make_async_copy(
            w_ref.at[pl.ds(j * width, width), :], w_buf.at[j % WBUFS], w_sem.at[j]
        )

    w_load(0).start()
    loads[2].start()
    loads[3].start()
    for j in range(1, WBUFS):
        w_load(j).start()

    barrier = pltpu.get_barrier_semaphore()
    for r in range(1, 4):
        pl.semaphore_signal(barrier, inc=1, device_id={"tensor": lax.rem(t + r, 4)}, device_id_type=MESH)

    @pl.when(is_mid)
    def _():
        pl.semaphore_signal(barrier, inc=1, device_id={"dp": outer}, device_id_type=MESH)
        pl.semaphore_signal(barrier, inc=1, device_id={"dp": cross}, device_id_type=MESH)
        pl.semaphore_wait(barrier, 5)

    @pl.when(is_end)
    def _():
        pl.semaphore_signal(barrier, inc=1, device_id={"dp": inner}, device_id_type=MESH)
        pl.semaphore_wait(barrier, 4)

    def remote(src, dst, ssem, rsem, dev):
        return pltpu.make_async_remote_copy(
            src_ref=src, dst_ref=dst, send_sem=ssem, recv_sem=rsem, device_id=dev, device_id_type=MESH
        )

    def rows_of(b):
        return pl.ds(pl.multiple_of(b * BLOCK, BLOCK), BLOCK)

    def hid_copy(r, sender):
        p = lax.rem(t + r, 4)
        return remote(
            hid_ref.at[:, pl.ds(pl.multiple_of(p * width, 128), width)],
            cols.at[rows_of(sender), :], hs_sem.at[r], hr_sem.at[r], {"tensor": p},
        )

    for r in range(1, 4):
        hid_copy(r, t).start()

    lane = lax.broadcasted_iota(jnp.int32, ids_s.shape, 1) // rank
    ids = jnp.zeros(ids_s.shape, F32)
    for b in range(nb):
        ids = ids + jnp.where(lane == b, 1.0, 0.0) * idx_ref[b].astype(F32)
    ids_s[...] = ids

    @pl.when(is_end)
    def _():
        remote(ids_s, ids_r, id_sem.at[0], id_sem.at[1], {"dp": inner}).start()

    loads[0].wait()
    loads[1].wait()
    for b in range(nb):
        keep = (lax.broadcasted_iota(jnp.int32, (BLOCK, 1), 0) < live_ref[b]).astype(F32)
        rows = (m_g[pl.ds(b * BLOCK, BLOCK), :].astype(F32) * keep).astype(BF16)
        m_g[pl.ds(b * BLOCK, BLOCK), :] = rows
        lg_s[:, pl.ds(b * BLOCK, BLOCK)] = dot_nt(up_v[idx_ref[b]], rows).astype(BF16)

    def low_copy(buf_s, buf_r, ssem, rsem, r):
        return remote(buf_s, buf_r.at[r - 1], ssem.at[r], rsem.at[r], {"tensor": lax.rem(t + r, 4)})

    for r in range(1, 4):
        low_copy(lg_s, lg_r, lgs_sem, lgr_sem, r).start()

    def partial(j):
        w_load(j).wait()

        def body(n, carry):
            at = pl.ds(pl.multiple_of(n * STEP, STEP), STEP)
            pf[j % 2, :, at] = dot_nt(m_g[...], w_buf[j % WBUFS, at, :])
            return carry

        lax.fori_loop(0, width // STEP, body, 0)
        if j + WBUFS < 4:
            w_load(j + WBUFS).start()

    def core_copy(j):
        return remote(core_s.at[j], core_r.at[j], cs_sem.at[j], cr_sem.at[j], {"tensor": core_peer})

    def y_copy(j):
        return remote(y_s.at[j], y_r.at[j], ys_sem.at[j], yr_sem.at[j], {"tensor": y_peer})

    def send_core(j):
        @pl.when(t == j)
        def _():
            for b in range(nb):
                at = pl.ds(b * BLOCK, BLOCK)
                pf[j % 2, at, :] = pf[j % 2, at, :] + lora[at, :].astype(F32)

        for k in range(2):
            core_s[j, k] = pf[j % 2, rows_of(2 * k + 1 - c), :].astype(BF16)
        core_copy(j).start()

    def combine(j):
        core_copy(j).wait_recv()
        y_s[j] = (pf[j % 2, rows_of((1 - y) * 2 + c), :] + core_r[j, 1 - y].astype(F32)).astype(BF16)
        y_copy(j).start()
        acc[:, pl.ds(j * width, width)] = pf[j % 2, rows_of(y * 2 + c), :] + core_r[j, y].astype(F32)

    partial(0)
    partial(1)

    for r in range(1, 4):
        low_copy(lg_s, lg_r, lgs_sem, lgr_sem, r).wait_recv()
    low_g[...] = (
        lg_s[...].astype(F32) + lg_r[0].astype(F32) + lg_r[1].astype(F32) + lg_r[2].astype(F32)
    ).astype(BF16)
    loads[3].wait()
    for b in range(nb):
        at = pl.ds(b * BLOCK, BLOCK)
        lora[at, :] = (adapter_scale * dot_tn(low_g[:, at], down_v[idx_ref[b]])).astype(BF16)
    send_core(0)
    send_core(1)

    loads[2].wait()
    for r in range(1, 4):
        hid_copy(r, lax.rem(t + 4 - r, 4)).wait_recv()
    for b in range(nb):
        at = pl.ds(b * BLOCK, BLOCK)
        la_s[:, at] = dot_nt(down_v[idx_ref[b]], cols[at, :]).astype(BF16)
    for r in range(1, 4):
        low_copy(la_s, la_r, las_sem, lar_sem, r).start()

    end_f = is_end.astype(F32)

    def adapter_of(s):
        if s < own:
            return cross * own + s
        if s < 2 * own:
            return far * own + (s - own)
        if s < 3 * own:
            return d * own + (s - 2 * own)
        return outer * own + (s - 3 * own)

    def fill(low):
        for s in range(4 * own):
            for b in range(nb):
                same = (idx_ref[b] == adapter_of(s)).astype(F32)
                if s < 2 * own:
                    same = end_f * (1.0 if s == b else 0.0) + (1.0 - end_f) * same
                at = pl.ds(b * BLOCK, BLOCK)
                lhs[pl.ds(s * rank, rank), at] = (low[:, at].astype(F32) * (adapter_scale * same)).astype(BF16)

    NC = DOWN_CHUNKS + UP_CHUNKS

    def pick(k, down, up):
        return down.at[k] if k < DOWN_CHUNKS else up.at[k - DOWN_CHUNKS]

    def slot_at(k):
        if k < DOWN_CHUNKS:
            return slots_d, pl.ds(k * dw, dw)
        return slots_u, pl.ds((k - DOWN_CHUNKS) * uw, uw)

    def end_copy(k):
        return remote(pick(k, s1d, s1u), pick(k, td, tu), s1_sem.at[k], t_sem.at[k], {"dp": inner})

    def cross_copy(k):
        return remote(pick(k, s1d, s1u), pick(k, xd, xu), s1_sem.at[k], x_sem.at[k], {"dp": cross})

    def outer_copy(k):
        return remote(pick(k, s2d, s2u), pick(k, fd, fu), s2_sem.at[k], f_sem.at[k], {"dp": outer})

    half, own_rows, out_rows = 2 * own * rank, own * rank, 3 * own * rank

    def local_terms(k):
        slots, at = slot_at(k)
        right = cols if k < DOWN_CHUNKS else m_g
        slots[:, at] = dot_nn(lhs[...], right[:, at])

        @pl.when(is_end)
        def _():
            pick(k, s1d, s1u)[...] = slots[0:half, at].astype(BF16)
            end_copy(k).start()

    def middle_sums(k):
        slots, at = slot_at(k)

        @pl.when(is_mid)
        def _():
            end_copy(k).wait_recv()
            more = dot_nn(sel[...], pick(k, td, tu)[...])
            pick(k, s1d, s1u)[...] = (slots[0:half, at] + more[0:half]).astype(BF16)
            cross_copy(k).start()
            slots[half:out_rows, at] = slots[half:out_rows, at] + more[half:]

    def middle_out(k):
        slots, at = slot_at(k)
        out = gd_ref if k < DOWN_CHUNKS else gu_ref

        @pl.when(is_mid)
        def _():
            cross_copy(k).wait_recv()
            got = pick(k, xd, xu)
            pick(k, s2d, s2u)[...] = (slots[out_rows:, at] + got[own_rows:, :].astype(F32)).astype(BF16)
            outer_copy(k).start()
            out[:, at] = slots[half:out_rows, at] + got[0:own_rows, :].astype(F32)

    def end_out(k):
        slots, at = slot_at(k)
        out = gd_ref if k < DOWN_CHUNKS else gu_ref

        @pl.when(is_end)
        def _():
            outer_copy(k).wait_recv()
            out[:, at] = slots[half:out_rows, at] + pick(k, fd, fu)[...].astype(F32)

    fill(low_g)
    for k in range(DOWN_CHUNKS):
        local_terms(k)
    combine(0)
    combine(1)
    partial(2)
    send_core(2)

    for r in range(1, 4):
        low_copy(la_s, la_r, las_sem, lar_sem, r).wait_recv()
    low_a[...] = (
        la_s[...].astype(F32) + la_r[0].astype(F32) + la_r[1].astype(F32) + la_r[2].astype(F32)
    ).astype(BF16)
    fill(low_a)
    for k in range(DOWN_CHUNKS, NC):
        local_terms(k)

    @pl.when(is_mid)
    def _():
        remote(ids_s, ids_r, id_sem.at[0], id_sem.at[1], {"dp": cross}).wait_recv()
        eye = lax.broadcasted_iota(jnp.int32, (rank, nb * rank), 0) == (
            lax.broadcasted_iota(jnp.int32, (rank, nb * rank), 1) % rank
        )
        eye = eye.astype(F32)
        for s in range(3 * own):
            same = (ids_r[0:1, :] == adapter_of(s).astype(F32)).astype(F32)
            sel[pl.ds(s * rank, rank), :] = (eye * same).astype(BF16)

    for k in range(DOWN_CHUNKS):
        middle_sums(k)
    combine(2)
    partial(3)
    send_core(3)
    middle_sums(DOWN_CHUNKS)
    combine(3)
    for k in range(DOWN_CHUNKS):
        middle_out(k)
    for k in range(DOWN_CHUNKS + 1, NC):
        middle_sums(k)
        middle_out(k - 1)
    middle_out(NC - 1)
    for j in range(4):
        at = pl.ds(j * width, width)
        y_copy(j).wait_recv()
        hg_ref[:, at] = (acc[:, at] + y_r[j].astype(F32)).astype(BF16)
    for k in range(NC):
        end_out(k)

    for r in range(1, 4):
        hid_copy(r, t).wait_send()
        low_copy(lg_s, lg_r, lgs_sem, lgr_sem, r).wait_send()
        low_copy(la_s, la_r, las_sem, lar_sem, r).wait_send()
    for j in range(4):
        core_copy(j).wait_send()
        y_copy(j).wait_send()
    for k in range(NC):
        end_copy(k).wait_send()

    @pl.when(is_mid)
    def _():
        for k in range(NC):
            outer_copy(k).wait_send()

    @pl.when(is_end)
    def _():
        remote(ids_s, ids_r, id_sem.at[0], id_sem.at[1], {"dp": inner}).wait_send()


def fused(hidden_input, query_gradient, weight, adapter_down, adapter_up, live_per_block, adapter_per_block):
    down_t = adapter_down.transpose(0, 2, 1)
    na, rank, width = down_t.shape
    group, q = query_gradient.shape
    rows, model = hidden_input.shape
    own = na // 4
    nt = 4
    uw, dw = q // UP_CHUNKS, width // DOWN_CHUNKS
    half, mine = 2 * own * rank, own * rank
    V, S = pltpu.VMEM, pltpu.SemaphoreType.DMA
    nc = UP_CHUNKS + DOWN_CHUNKS

    def pair(height):
        return [V((DOWN_CHUNKS, height, dw), BF16), V((UP_CHUNKS, height, uw), BF16)]

    any_spec = pl.BlockSpec(memory_space=pl.ANY)
    smem = pl.BlockSpec(memory_space=pltpu.SMEM)
    vmem = pl.BlockSpec(memory_space=pltpu.VMEM)
    hg, gd, gu = pl.pallas_call(
        kernel,
        out_shape=(
            jax.ShapeDtypeStruct((rows, model), BF16),
            jax.ShapeDtypeStruct((mine, width), F32),
            jax.ShapeDtypeStruct((mine, q), F32),
        ),
        in_specs=[smem, smem] + [any_spec] * 5,
        out_specs=(vmem,) * 3,
        scratch_shapes=[
            V((group, q), BF16),
            V((WBUFS, width, q), BF16),
            V((na, rank, q), BF16),
            V((na, rank, width), BF16),
            V((group, width), BF16),
            V((2, group, width), F32),
            V((rows, model), F32),
            V((nt, 2, rows, width), BF16),
            V((nt, 2, rows, width), BF16),
            V((nt, rows, width), BF16),
            V((nt, rows, width), BF16),
            V((group, width), BF16),
            V((rank, group), BF16),
            V((3, rank, group), BF16),
            V((rank, group), BF16),
            V((3, rank, group), BF16),
            V((rank, group), BF16),
            V((rank, group), BF16),
            V((na * rank, group), BF16),
            V((na * rank, width), F32),
            V((na * rank, q), F32),
        ]
        + pair(half) + pair(half) + pair(half) + pair(mine) + pair(mine)
        + [V((8, nt * rank), F32), V((8, nt * rank), F32), V((3 * mine, nt * rank), BF16)]
        + [S((n,)) for n in (4, 4, 4, 4, 4, 4, 4, 4, 4, 4, 4, 4, nc, nc, nc, nc, nc, 2)],
        compiler_params=pltpu.CompilerParams(
            collective_id=0, has_side_effects=True, vmem_limit_bytes=62 * 1024 * 1024
        ),
        cost_estimate=pl.CostEstimate(
            flops=2 * group * q * model, bytes_accessed=2 * model * q, transcendentals=0
        ),
    )(
        live_per_block, adapter_per_block[:, 0], hidden_input, query_gradient, weight, down_t, adapter_up,
    )
    return hg, gd.reshape(own, rank, width).transpose(0, 2, 1), gu.reshape(own, rank, q)


def on_device(
    hidden_input,
    query_gradient,
    weight,
    adapter_down,
    adapter_up,
    live_per_block,
    adapter_per_block,
):
    token_rows_local = hidden_input.shape[0]
    group = query_gradient.shape[0]
    nblocks = group // BLOCK
    q_local = query_gradient.shape[1]
    local_width = adapter_down.shape[1]
    adapter_list = adapter_down.shape[0]
    positions = jnp.arange(BLOCK, dtype=jnp.int32)
    live = (positions[None, :] < live_per_block[:, None]).astype(jnp.bfloat16)
    masked_rows = query_gradient.reshape(nblocks, BLOCK, q_local) * live[:, :, None]
    adapter_index = adapter_per_block[:, 0]
    columns = lax.all_to_all(hidden_input, "tensor", split_axis=1, concat_axis=0, tiled=True)
    column_blocks = columns.reshape(nblocks, BLOCK, local_width)
    down_block_list = adapter_down[adapter_index]
    up_block_list = adapter_up[adapter_index]
    grad_part = jnp.einsum(
        "bkq,brq->bkr", masked_rows, up_block_list, preferred_element_type=jnp.float32
    )
    act_part = jnp.einsum(
        "shu,sup->shp", column_blocks, down_block_list, preferred_element_type=jnp.float32
    )
    grad_sum, act_sum = (
        lax.psum(grad_part.astype(jnp.bfloat16), "tensor").astype(jnp.float32),
        lax.psum(act_part.astype(jnp.bfloat16), "tensor").astype(jnp.float32),
    )
    rank_gradient = grad_sum.astype(jnp.bfloat16)
    act_low = act_sum.astype(jnp.bfloat16)
    flat = masked_rows.reshape(group, q_local)
    frozen_gradient = lax.psum_scatter(
        lax.dot_general(
            flat, weight, (((1,), (1,)), ((), ())), preferred_element_type=jnp.float32
        ).astype(jnp.bfloat16),
        "tensor",
        scatter_dimension=0,
        tiled=True,
    ).astype(jnp.float32)
    complete_down = lax.all_gather(adapter_down, "tensor", axis=1, tiled=True)
    own_count = token_rows_local // BLOCK
    first = lax.axis_index("tensor") * own_count
    local_gradient = lax.dynamic_slice_in_dim(rank_gradient, first, own_count, 0)
    local_index = lax.dynamic_slice_in_dim(adapter_index, first, own_count, 0)
    local_rows = adapter_scale * jnp.einsum(
        "lqm,lsm->lqs",
        local_gradient,
        complete_down[local_index],
        preferred_element_type=jnp.float32,
    )
    adapter_rows = local_rows.astype(jnp.bfloat16).reshape(token_rows_local, hidden_input.shape[1])
    hidden_gradient = (frozen_gradient + adapter_rows.astype(jnp.float32)).astype(jnp.bfloat16)
    down_terms = jnp.einsum(
        "mfq,mfc->mqc", column_blocks, rank_gradient, preferred_element_type=jnp.float32
    )
    up_terms = jnp.einsum("bkr,bkq->brq", act_low, masked_rows, preferred_element_type=jnp.float32)
    selector = (
        adapter_index[None, :] == jnp.arange(adapter_list, dtype=jnp.int32)[:, None]
    ).astype(jnp.float32)
    down_total = adapter_scale * jnp.einsum(
        "ab,bdr->adr", selector, down_terms, precision=lax.Precision.HIGHEST
    )
    up_total = adapter_scale * jnp.einsum(
        "ab,brq->arq", selector, up_terms, precision=lax.Precision.HIGHEST
    )
    grad_down, grad_up = (
        lax.psum_scatter(
            down_total.astype(jnp.bfloat16), "dp", scatter_dimension=0, tiled=True
        ).astype(jnp.float32),
        lax.psum_scatter(
            up_total.astype(jnp.bfloat16), "dp", scatter_dimension=0, tiled=True
        ).astype(jnp.float32),
    )
    return (hidden_gradient, grad_down, grad_up)


def solution(mesh):
    sizes = (mesh.shape["dp"], mesh.shape["tensor"])
    return jax.shard_map(
        fused if sizes == (4, 4) else on_device,
        mesh=mesh,
        in_specs=(
            P(("groups", "dp", "tensor"), None),
            P(("groups", "dp"), "tensor"),
            P(None, "tensor"),
            P(None, "tensor", None),
            P(None, None, "tensor"),
            P(("groups", "dp")),
            P(("groups", "dp"), None),
        ),
        out_specs=(
            P(("groups", "dp", "tensor"), None),
            P(("groups", "dp"), "tensor", None),
            P(("groups", "dp"), None, "tensor"),
        ),
        check_vma=False,
    )
```

```python
import jax
import jax.numpy as jnp
from jax import lax
from jax.experimental import pallas as pl
from jax.experimental.pallas import tpu as pltpu
from jax.sharding import PartitionSpec as P

BLOCK = 128
MESH = pl.DeviceIdType.MESH
F32, BF16 = jnp.float32, jnp.bfloat16


adapter_scale = 2.0
UP_CHUNKS, DOWN_CHUNKS, STEP, WBUFS = 8, 5, 256, 3


def dot_nt(a, b):
    return lax.dot_general(a, b, (((1,), (1,)), ((), ())), preferred_element_type=F32)


def dot_nn(a, b):
    return lax.dot_general(a, b, (((1,), (0,)), ((), ())), preferred_element_type=F32)


def dot_tn(a, b):
    return lax.dot_general(a, b, (((0,), (0,)), ((), ())), preferred_element_type=F32)


def kernel(
    live_ref, idx_ref, hid_ref, g_ref, w_ref, down_ref, up_ref,
    hg_ref, gd_ref, gu_ref,
    m_g, w_buf, up_v, down_v, hid_v, d_s, d_r, term_s, term_r, pf, acc, core_s, core_r, y_s, y_r, lora,
    lg_s, lg_r, la_r, low_g, low_a, lhs, lhs_d, slots_d, slots_u,
    s1d, s1u, td, tu, xd, xu, s2d, s2u, fd, fu, ids_s, ids_r, sel,
    loc_sem, w_sem, hs_sem, hr_sem, ts_sem, tr_sem, lgs_sem, lgr_sem, las_sem, lar_sem,
    cs_sem, cr_sem, ys_sem, yr_sem,
    s1_sem, t_sem, x_sem, s2_sem, f_sem, id_sem,
):
    d = lax.axis_index("dp")
    t = lax.axis_index("tensor")
    y, c = t // 2, t % 2
    core_peer = y * 2 + (1 - c)
    y_peer = (1 - y) * 2 + c
    is_mid = jnp.logical_or(d == 1, d == 2)
    is_end = jnp.logical_not(is_mid)
    low_side = d < 2
    outer = jnp.where(low_side, 0, 3)
    inner = jnp.where(low_side, 1, 2)
    cross = jnp.where(low_side, 2, 1)
    far = 3 - outer
    nb = 4
    own, rank = gd_ref.shape[0] // 64, 64
    width = down_v.shape[2]
    q = m_g.shape[1]
    uw, dw = q // UP_CHUNKS, width // DOWN_CHUNKS

    loads = [
        pltpu.make_async_copy(g_ref, m_g, loc_sem.at[0]),
        pltpu.make_async_copy(up_ref, up_v, loc_sem.at[1]),
        pltpu.make_async_copy(hid_ref, hid_v, loc_sem.at[2]),
        pltpu.make_async_copy(down_ref, down_v, loc_sem.at[3]),
    ]
    for x in (loads[3], loads[0], loads[1], loads[2]):
        x.start()

    def w_load(j):
        return pltpu.make_async_copy(
            w_ref.at[pl.ds(j * width, width), :], w_buf.at[j % WBUFS], w_sem.at[j]
        )

    w_load(0).start()
    for j in range(1, WBUFS):
        w_load(j).start()

    barrier = pltpu.get_barrier_semaphore()
    for r in range(1, 4):
        pl.semaphore_signal(barrier, inc=1, device_id={"tensor": lax.rem(t + r, 4)}, device_id_type=MESH)

    @pl.when(is_mid)
    def _():
        pl.semaphore_signal(barrier, inc=1, device_id={"dp": outer}, device_id_type=MESH)
        pl.semaphore_signal(barrier, inc=1, device_id={"dp": cross}, device_id_type=MESH)
        pl.semaphore_wait(barrier, 5)

    @pl.when(is_end)
    def _():
        pl.semaphore_signal(barrier, inc=1, device_id={"dp": inner}, device_id_type=MESH)
        pl.semaphore_wait(barrier, 4)

    def remote(src, dst, ssem, rsem, dev):
        return pltpu.make_async_remote_copy(
            src_ref=src, dst_ref=dst, send_sem=ssem, recv_sem=rsem, device_id=dev, device_id_type=MESH
        )

    def rows_of(b):
        return pl.ds(pl.multiple_of(b * BLOCK, BLOCK), BLOCK)

    def down_copy(r):
        return remote(d_s.at[r - 1], d_r.at[r - 1], hs_sem.at[r], hr_sem.at[r], {"tensor": lax.rem(t + r, 4)})

    def term_copy(r, sender):
        return remote(
            term_s.at[r - 1], term_r.at[sender], ts_sem.at[r], tr_sem.at[r], {"tensor": lax.rem(t + r, 4)}
        )

    loads[3].wait()
    for r in (2, 3, 1):
        d_s[r - 1] = down_v[idx_ref[lax.rem(t + r, 4)]]
        down_copy(r).start()

    lane = lax.broadcasted_iota(jnp.int32, ids_s.shape, 1) // rank
    ids = jnp.zeros(ids_s.shape, F32)
    for b in range(nb):
        ids = ids + jnp.where(lane == b, 1.0, 0.0) * idx_ref[b].astype(F32)
    ids_s[...] = ids

    @pl.when(is_end)
    def _():
        remote(ids_s, ids_r, id_sem.at[0], id_sem.at[1], {"dp": inner}).start()

    loads[0].wait()
    loads[1].wait()
    for b in range(nb):
        keep = (lax.broadcasted_iota(jnp.int32, (BLOCK, 1), 0) < live_ref[b]).astype(F32)
        rows = (m_g[pl.ds(b * BLOCK, BLOCK), :].astype(F32) * keep).astype(BF16)
        m_g[pl.ds(b * BLOCK, BLOCK), :] = rows
        lg_s[:, pl.ds(b * BLOCK, BLOCK)] = dot_nt(up_v[idx_ref[b]], rows).astype(BF16)

    def low_copy(buf_s, buf_r, ssem, rsem, r):
        return remote(buf_s, buf_r.at[r - 1], ssem.at[r], rsem.at[r], {"tensor": lax.rem(t + r, 4)})

    for r in range(1, 4):
        low_copy(lg_s, lg_r, lgs_sem, lgr_sem, r).start()

    def partial(j, begin=0, end=None):
        last = width // STEP
        end = last if end is None else end
        if begin == 0:
            w_load(j).wait()

        def body(n, carry):
            at = pl.ds(pl.multiple_of(n * STEP, STEP), STEP)
            pf[j % 2, :, at] = dot_nt(m_g[...], w_buf[j % WBUFS, at, :])
            return carry

        lax.fori_loop(begin, end, body, 0)
        if end == last and j + WBUFS < 4:
            w_load(j + WBUFS).start()

    def core_copy(j):
        return remote(core_s.at[j], core_r.at[j], cs_sem.at[j], cr_sem.at[j], {"tensor": core_peer})

    def y_copy(j):
        return remote(y_s.at[j], y_r.at[j], ys_sem.at[j], yr_sem.at[j], {"tensor": y_peer})

    def send_core(j):
        @pl.when(t == j)
        def _():
            for b in range(nb):
                at = pl.ds(b * BLOCK, BLOCK)
                pf[j % 2, at, :] = pf[j % 2, at, :] + lora[at, :].astype(F32)

        for k in range(2):
            core_s[j, k] = pf[j % 2, rows_of(2 * k + 1 - c), :].astype(BF16)
        core_copy(j).start()

    def combine(j):
        core_copy(j).wait_recv()
        y_s[j] = (pf[j % 2, rows_of((1 - y) * 2 + c), :] + core_r[j, 1 - y].astype(F32)).astype(BF16)
        y_copy(j).start()
        acc[:, pl.ds(j * width, width)] = pf[j % 2, rows_of(y * 2 + c), :] + core_r[j, y].astype(F32)

    partial(0)

    def hid_cols(p):
        return hid_v[:, pl.ds(pl.multiple_of(p * width, 128), width)]

    loads[2].wait()
    mine = dot_nt(down_v[idx_ref[t]], hid_cols(t))
    for r in range(1, 4):
        down_copy(r).wait_recv()
        mine = mine + dot_nt(d_r[r - 1], hid_cols(lax.rem(t + 4 - r, 4)))
    low_a[:, rows_of(t)] = mine.astype(BF16)

    def act_copy(r):
        return remote(
            low_a.at[:, rows_of(t)], la_r.at[r - 1], las_sem.at[r], lar_sem.at[r], {"tensor": lax.rem(t + r, 4)}
        )

    for r in range(1, 4):
        act_copy(r).start()

    for r in range(1, 4):
        low_copy(lg_s, lg_r, lgs_sem, lgr_sem, r).wait_recv()
    low_g[...] = (
        lg_s[...].astype(F32) + lg_r[0].astype(F32) + lg_r[1].astype(F32) + lg_r[2].astype(F32)
    ).astype(BF16)
    own_low = (adapter_scale * low_g[:, rows_of(t)].astype(F32)).astype(BF16)
    for r in (2, 3, 1):
        term_s[r - 1] = dot_nn(own_low, hid_cols(lax.rem(t + r, 4))).astype(BF16)
        term_copy(r, t).start()
    term_r[t] = dot_nn(own_low, hid_cols(t)).astype(BF16)

    end_f = is_end.astype(F32)

    def adapter_of(s):
        if s < own:
            return cross * own + s
        if s < 2 * own:
            return far * own + (s - own)
        if s < 3 * own:
            return d * own + (s - 2 * own)
        return outer * own + (s - 3 * own)

    def share(s, b):
        same = (idx_ref[b] == adapter_of(s)).astype(F32)
        if s < 2 * own:
            same = end_f * (1.0 if s == b else 0.0) + (1.0 - end_f) * same
        return same

    eye = (
        lax.broadcasted_iota(jnp.int32, (rank, nb * rank), 0)
        == lax.broadcasted_iota(jnp.int32, (rank, nb * rank), 1) % rank
    ).astype(F32)
    owner = lax.broadcasted_iota(jnp.int32, (1, nb * rank), 1) // rank

    def fill_up():
        for s in range(4 * own):
            for b in range(nb):
                at = pl.ds(b * BLOCK, BLOCK)
                lhs[pl.ds(s * rank, rank), at] = (
                    low_a[:, at].astype(F32) * (adapter_scale * share(s, b))
                ).astype(BF16)

    def fill_down():
        for s in range(4 * own):
            row = jnp.zeros((1, nb * rank), F32)
            for b in range(nb):
                row = row + (owner == b).astype(F32) * share(s, b)
            lhs_d[pl.ds(s * rank, rank), :] = (eye * row).astype(BF16)

    NC = DOWN_CHUNKS + UP_CHUNKS

    def pick(k, down, up):
        return down.at[k - UP_CHUNKS] if k >= UP_CHUNKS else up.at[k]

    def slot_at(k):
        if k >= UP_CHUNKS:
            return slots_d, pl.ds((k - UP_CHUNKS) * dw, dw)
        return slots_u, pl.ds(k * uw, uw)

    def end_copy(k):
        return remote(pick(k, s1d, s1u), pick(k, td, tu), s1_sem.at[k], t_sem.at[k], {"dp": inner})

    def cross_copy(k):
        return remote(pick(k, s1d, s1u), pick(k, xd, xu), s1_sem.at[k], x_sem.at[k], {"dp": cross})

    def outer_copy(k):
        return remote(pick(k, s2d, s2u), pick(k, fd, fu), s2_sem.at[k], f_sem.at[k], {"dp": outer})

    half, own_rows, out_rows = 2 * own * rank, own * rank, 3 * own * rank

    def local_terms(k):
        slots, at = slot_at(k)
        if k >= UP_CHUNKS:
            right = jnp.concatenate([term_r[b, :, at] for b in range(nb)], axis=0)
            slots[:, at] = dot_nn(lhs_d[...], right)
        else:
            slots[:, at] = dot_nn(lhs[...], m_g[:, at])

        @pl.when(is_end)
        def _():
            pick(k, s1d, s1u)[...] = slots[0:half, at].astype(BF16)
            end_copy(k).start()

    def middle_sums(k):
        slots, at = slot_at(k)

        @pl.when(is_mid)
        def _():
            end_copy(k).wait_recv()
            more = dot_nn(sel[...], pick(k, td, tu)[...])
            pick(k, s1d, s1u)[...] = (slots[0:half, at] + more[0:half]).astype(BF16)
            cross_copy(k).start()
            slots[half:out_rows, at] = slots[half:out_rows, at] + more[half:]

    def middle_out(k):
        slots, at = slot_at(k)
        out = gd_ref if k >= UP_CHUNKS else gu_ref

        @pl.when(is_mid)
        def _():
            cross_copy(k).wait_recv()
            got = pick(k, xd, xu)
            pick(k, s2d, s2u)[...] = (slots[out_rows:, at] + got[own_rows:, :].astype(F32)).astype(BF16)
            outer_copy(k).start()
            out[:, at] = slots[half:out_rows, at] + got[0:own_rows, :].astype(F32)

    def end_out(k):
        slots, at = slot_at(k)
        out = gd_ref if k >= UP_CHUNKS else gu_ref

        @pl.when(is_end)
        def _():
            outer_copy(k).wait_recv()
            out[:, at] = slots[half:out_rows, at] + pick(k, fd, fu)[...].astype(F32)

    for r in range(1, 4):
        act_copy(r).wait_recv()
        low_a[:, rows_of(lax.rem(t + 4 - r, 4))] = la_r[r - 1]
    fill_up()
    for k in range(UP_CHUNKS):
        local_terms(k)

    @pl.when(is_mid)
    def _():
        remote(ids_s, ids_r, id_sem.at[0], id_sem.at[1], {"dp": cross}).wait_recv()
        for s in range(3 * own):
            same = (ids_r[0:1, :] == adapter_of(s).astype(F32)).astype(F32)
            sel[pl.ds(s * rank, rank), :] = (eye * same).astype(BF16)

    for b in range(nb):
        at = pl.ds(b * BLOCK, BLOCK)
        lora[at, :] = (adapter_scale * dot_tn(low_g[:, at], down_v[idx_ref[b]])).astype(BF16)
    send_core(0)
    middle_sums(0)
    partial(1, 0, 3)
    middle_sums(1)
    partial(1, 3)
    send_core(1)
    combine(0)
    middle_sums(2)
    fill_down()
    for r in range(1, 4):
        term_copy(r, lax.rem(t + 4 - r, 4)).wait_recv()
    for k in range(UP_CHUNKS, NC):
        local_terms(k)
    middle_sums(3)
    middle_out(0)
    partial(2, 0, 3)
    middle_sums(4)
    middle_out(1)
    combine(1)
    partial(2, 3)
    send_core(2)
    middle_sums(5)
    middle_out(2)
    partial(3, 0, 3)
    middle_sums(6)
    middle_out(3)
    combine(2)
    partial(3, 3)
    send_core(3)
    middle_sums(7)
    middle_out(4)
    combine(3)
    for k in range(UP_CHUNKS, NC):
        middle_sums(k)
        middle_out(k - 3)
    for k in range(NC - 3, NC):
        middle_out(k)
    for j in range(4):
        at = pl.ds(j * width, width)
        y_copy(j).wait_recv()
        hg_ref[:, at] = (acc[:, at] + y_r[j].astype(F32)).astype(BF16)
    for k in range(NC):
        end_out(k)

    for r in range(1, 4):
        down_copy(r).wait_send()
        term_copy(r, t).wait_send()
        low_copy(lg_s, lg_r, lgs_sem, lgr_sem, r).wait_send()
        act_copy(r).wait_send()
    for j in range(4):
        core_copy(j).wait_send()
        y_copy(j).wait_send()
    for k in range(NC):
        end_copy(k).wait_send()

    @pl.when(is_mid)
    def _():
        for k in range(NC):
            outer_copy(k).wait_send()

    @pl.when(is_end)
    def _():
        remote(ids_s, ids_r, id_sem.at[0], id_sem.at[1], {"dp": inner}).wait_send()


def fused(hidden_input, query_gradient, weight, adapter_down, adapter_up, live_per_block, adapter_per_block):
    down_t = adapter_down.transpose(0, 2, 1)
    na, rank, width = down_t.shape
    group, q = query_gradient.shape
    rows, model = hidden_input.shape
    own = na // 4
    nt = 4
    uw, dw = q // UP_CHUNKS, width // DOWN_CHUNKS
    half, mine = 2 * own * rank, own * rank
    V, S = pltpu.VMEM, pltpu.SemaphoreType.DMA
    nc = UP_CHUNKS + DOWN_CHUNKS

    def pair(height):
        return [V((DOWN_CHUNKS, height, dw), BF16), V((UP_CHUNKS, height, uw), BF16)]

    any_spec = pl.BlockSpec(memory_space=pl.ANY)
    smem = pl.BlockSpec(memory_space=pltpu.SMEM)
    vmem = pl.BlockSpec(memory_space=pltpu.VMEM)
    hg, gd, gu = pl.pallas_call(
        kernel,
        out_shape=(
            jax.ShapeDtypeStruct((rows, model), BF16),
            jax.ShapeDtypeStruct((mine, width), F32),
            jax.ShapeDtypeStruct((mine, q), F32),
        ),
        in_specs=[smem, smem] + [any_spec] * 5,
        out_specs=(vmem,) * 3,
        scratch_shapes=[
            V((group, q), BF16),
            V((WBUFS, width, q), BF16),
            V((na, rank, q), BF16),
            V((na, rank, width), BF16),
            V((rows, model), BF16),
            V((3, rank, width), BF16),
            V((3, rank, width), BF16),
            V((3, rank, width), BF16),
            V((nt, rank, width), BF16),
            V((2, group, width), F32),
            V((rows, model), F32),
            V((nt, 2, rows, width), BF16),
            V((nt, 2, rows, width), BF16),
            V((nt, rows, width), BF16),
            V((nt, rows, width), BF16),
            V((group, width), BF16),
            V((rank, group), BF16),
            V((3, rank, group), BF16),
            V((3, rank, rows), BF16),
            V((rank, group), BF16),
            V((rank, group), BF16),
            V((na * rank, group), BF16),
            V((na * rank, nt * rank), BF16),
            V((na * rank, width), F32),
            V((na * rank, q), F32),
        ]
        + pair(half) + pair(half) + pair(half) + pair(mine) + pair(mine)
        + [V((8, nt * rank), F32), V((8, nt * rank), F32), V((3 * mine, nt * rank), BF16)]
        + [S((n,)) for n in (4, 4, 4, 4, 4, 4, 4, 4, 4, 4, 4, 4, 4, 4, nc, nc, nc, nc, nc, 2)],
        compiler_params=pltpu.CompilerParams(
            collective_id=0, has_side_effects=True, vmem_limit_bytes=62 * 1024 * 1024
        ),
        cost_estimate=pl.CostEstimate(
            flops=2 * group * q * model, bytes_accessed=2 * model * q, transcendentals=0
        ),
    )(
        live_per_block, adapter_per_block[:, 0], hidden_input, query_gradient, weight, down_t, adapter_up,
    )
    return hg, gd.reshape(own, rank, width).transpose(0, 2, 1), gu.reshape(own, rank, q)


def on_device(
    hidden_input,
    query_gradient,
    weight,
    adapter_down,
    adapter_up,
    live_per_block,
    adapter_per_block,
):
    token_rows_local = hidden_input.shape[0]
    group = query_gradient.shape[0]
    nblocks = group // BLOCK
    q_local = query_gradient.shape[1]
    local_width = adapter_down.shape[1]
    adapter_list = adapter_down.shape[0]
    positions = jnp.arange(BLOCK, dtype=jnp.int32)
    live = (positions[None, :] < live_per_block[:, None]).astype(jnp.bfloat16)
    masked_rows = query_gradient.reshape(nblocks, BLOCK, q_local) * live[:, :, None]
    adapter_index = adapter_per_block[:, 0]
    columns = lax.all_to_all(hidden_input, "tensor", split_axis=1, concat_axis=0, tiled=True)
    column_blocks = columns.reshape(nblocks, BLOCK, local_width)
    down_block_list = adapter_down[adapter_index]
    up_block_list = adapter_up[adapter_index]
    grad_part = jnp.einsum(
        "bkq,brq->bkr", masked_rows, up_block_list, preferred_element_type=jnp.float32
    )
    act_part = jnp.einsum(
        "shu,sup->shp", column_blocks, down_block_list, preferred_element_type=jnp.float32
    )
    grad_sum, act_sum = (
        lax.psum(grad_part.astype(jnp.bfloat16), "tensor").astype(jnp.float32),
        lax.psum(act_part.astype(jnp.bfloat16), "tensor").astype(jnp.float32),
    )
    rank_gradient = grad_sum.astype(jnp.bfloat16)
    act_low = act_sum.astype(jnp.bfloat16)
    flat = masked_rows.reshape(group, q_local)
    frozen_gradient = lax.psum_scatter(
        lax.dot_general(
            flat, weight, (((1,), (1,)), ((), ())), preferred_element_type=jnp.float32
        ).astype(jnp.bfloat16),
        "tensor",
        scatter_dimension=0,
        tiled=True,
    ).astype(jnp.float32)
    complete_down = lax.all_gather(adapter_down, "tensor", axis=1, tiled=True)
    own_count = token_rows_local // BLOCK
    first = lax.axis_index("tensor") * own_count
    local_gradient = lax.dynamic_slice_in_dim(rank_gradient, first, own_count, 0)
    local_index = lax.dynamic_slice_in_dim(adapter_index, first, own_count, 0)
    local_rows = adapter_scale * jnp.einsum(
        "lqm,lsm->lqs",
        local_gradient,
        complete_down[local_index],
        preferred_element_type=jnp.float32,
    )
    adapter_rows = local_rows.astype(jnp.bfloat16).reshape(token_rows_local, hidden_input.shape[1])
    hidden_gradient = (frozen_gradient + adapter_rows.astype(jnp.float32)).astype(jnp.bfloat16)
    down_terms = jnp.einsum(
        "mfq,mfc->mqc", column_blocks, rank_gradient, preferred_element_type=jnp.float32
    )
    up_terms = jnp.einsum("bkr,bkq->brq", act_low, masked_rows, preferred_element_type=jnp.float32)
    selector = (
        adapter_index[None, :] == jnp.arange(adapter_list, dtype=jnp.int32)[:, None]
    ).astype(jnp.float32)
    down_total = adapter_scale * jnp.einsum(
        "ab,bdr->adr", selector, down_terms, precision=lax.Precision.HIGHEST
    )
    up_total = adapter_scale * jnp.einsum(
        "ab,brq->arq", selector, up_terms, precision=lax.Precision.HIGHEST
    )
    grad_down, grad_up = (
        lax.psum_scatter(
            down_total.astype(jnp.bfloat16), "dp", scatter_dimension=0, tiled=True
        ).astype(jnp.float32),
        lax.psum_scatter(
            up_total.astype(jnp.bfloat16), "dp", scatter_dimension=0, tiled=True
        ).astype(jnp.float32),
    )
    return (hidden_gradient, grad_down, grad_up)


def solution(mesh):
    sizes = (mesh.shape["dp"], mesh.shape["tensor"])
    return jax.shard_map(
        fused if sizes == (4, 4) else on_device,
        mesh=mesh,
        in_specs=(
            P(("groups", "dp", "tensor"), None),
            P(("groups", "dp"), "tensor"),
            P(None, "tensor"),
            P(None, "tensor", None),
            P(None, None, "tensor"),
            P(("groups", "dp")),
            P(("groups", "dp"), None),
        ),
        out_specs=(
            P(("groups", "dp", "tensor"), None),
            P(("groups", "dp"), "tensor", None),
            P(("groups", "dp"), None, "tensor"),
        ),
        check_vma=False,
    )
```
